32 devices in a mesh: blk: 32 (over z, y, x, core).
Axes of the slice: x: 2, y: 2, z: 4, core: 2. Of those that a mesh axis runs over, the one named last changes fastest.
Arguments:
- positive_row: float32 [256, 8192], P(None, 'blk'), may hold values from -6 to 160, as said below
- negative_row: float32 [256, 8192], P(None, 'blk'), may hold values from -5 to 5
Outputs:
- positive_out: float32 [256, 8192], P(None, 'blk')
- negative_out: float32 [256, 8192], P(None, 'blk')
The draws below stay inside these ranges and needn't reach their ends.
Inputs may be any that keep to these rules, and one draw needn't show every extreme that they name: `positive_row`: the first 256 columns form an upper triangular block whose diagonal lies between 80 and 160.
All inputs are finite; a program needn't handle non-finite values.
Results may differ from the reference program's by a relative error of at most 0.00017.
Values sent between devices are 32-bit elements; how exact they have to be, the bound alone decides.
A program may use at most 64 MiB of HBM per device.

```python
import math
import jax
import jax.numpy as jnp
from jax import lax

B = 256
STEPS = 2
NEWTON = 4
ORDER = 8192


def draw_positive_row(key, part):
    key_bulk = jax.random.fold_in(key, 11)
    key_upper = jax.random.fold_in(key, 23)
    key_diag = jax.random.fold_in(key, 37)
    bulk = jnp.clip(0.4 * jax.random.normal(key_bulk, (B, ORDER), jnp.float32), -2.0, 2.0)
    upper = jnp.clip(0.6 * jax.random.normal(key_upper, (B, B), jnp.float32), -2.4, 2.4)
    diagonal = jnp.exp(jax.random.uniform(key_diag, (B,), jnp.float32, math.log(80.0), math.log(160.0)))
    rows_index = jnp.arange(B)[:, None]
    cols_index = jnp.arange(B)[None, :]
    leading = jnp.where(rows_index < cols_index, upper, 0.0) + jnp.where(rows_index == cols_index, diagonal[None, :], 0.0)
    return jnp.concatenate([leading, bulk[:, B:]], axis=1)


def levels(stream_key, extent, pieces, smallest, high):
    def one(axis_at, parts):
        draws = jax.random.uniform(jax.random.fold_in(jax.random.fold_in(stream_key, 6), axis_at), (parts,), jnp.float32, smallest / len(pieces), high / len(pieces))
        return jnp.repeat(jnp.exp(draws), extent[axis_at] // parts).reshape((-1,) + (1,) * (len(extent) - axis_at - 1))

    factor_of = one(*pieces[0])
    for cut in pieces[1:]:
        factor_of = factor_of * one(*cut)
    return factor_of


def normal_values(rng, dims, width, bound, shards=(), kind=jnp.bfloat16):
    entries = jax.random.normal(rng, dims, jnp.float32) * width
    if len(shards) > 0:
        entries = levels(rng, dims, shards, -0.22, 0.18) * entries
    return jnp.clip(entries, min=-bound, max=bound).astype(kind)


def setup_inputs(seed: int = 0) -> dict:
    key_list = jax.random.split(jax.random.key(seed), 3)
    positive_row = draw_positive_row(jax.random.fold_in(key_list[2], 71), 0)
    negative_row = normal_values(key_list[1], (B, ORDER), 0.4, 5.0, ((1, 32),), jnp.float32)
    return dict(positive_row=positive_row, negative_row=negative_row)


HIGHEST = lax.Precision.HIGHEST


def identity_of(size):
    rows_index = lax.broadcasted_iota(jnp.int32, (size, size), 0)
    cols_index = lax.broadcasted_iota(jnp.int32, (size, size), 1)
    return jnp.where(rows_index == cols_index, 1.0, 0.0).astype(jnp.float32)


def root_series(gram_part, identity):
    inner = 0.3125 * identity + 0.2734375 * gram_part
    inner = 0.375 * identity + jnp.dot(gram_part, inner, precision=HIGHEST)
    inner = 0.5 * identity + jnp.dot(gram_part, inner, precision=HIGHEST)
    return identity + jnp.dot(gram_part, inner, precision=HIGHEST)


def build_reflector(lead_p, lead_n):
    identity = identity_of(lead_p.shape[0])
    diag_values = jnp.sum(lead_p * identity, axis=1)
    approx = identity * (1.0 / diag_values)[:, None]
    lead_t = lead_p.T
    for newton_index in range(NEWTON):
        product = jnp.dot(lead_t, approx, precision=HIGHEST)
        approx = jnp.dot(approx, 2.0 * identity - product, precision=HIGHEST)
    coupling_t = jnp.dot(approx, lead_n.T, precision=HIGHEST)
    gram_top = jnp.dot(coupling_t, coupling_t.T, precision=HIGHEST)
    gram_bottom = jnp.dot(coupling_t.T, coupling_t, precision=HIGHEST)
    return coupling_t, root_series(gram_top, identity), root_series(gram_bottom, identity)


def apply_reflector(coupling_t, root_top, root_bottom, positive, negative):
    wide_p = positive - jnp.dot(coupling_t, negative, precision=HIGHEST)
    wide_n = negative - jnp.dot(coupling_t.T, positive, precision=HIGHEST)
    new_p = jnp.dot(root_top, wide_p, precision=HIGHEST)
    new_n = jnp.dot(root_bottom, wide_n, precision=HIGHEST)
    return new_p, new_n


def reference(positive_row, negative_row):
    positive = positive_row
    negative = negative_row
    for step_index in range(STEPS):
        lead_p = positive[:, step_index * B:(step_index + 1) * B]
        lead_n = negative[:, step_index * B:(step_index + 1) * B]
        coupling_t, root_top, root_bottom = build_reflector(lead_p, lead_n)
        new_p, new_n = apply_reflector(coupling_t, root_top, root_bottom, positive, negative)
        positive = jnp.concatenate([jnp.zeros((B, B), jnp.float32), new_p[:, :-B]], axis=1)
        negative = new_n
    return positive, negative
```

```python
import functools

import jax
import jax.numpy as jnp
from jax import lax
from jax.experimental import pallas as pl
from jax.experimental.pallas import tpu as pltpu
from jax.sharding import PartitionSpec as P

STEPS = 2
NEWTON = 4
CHUNKS = 4
MESH = pl.DeviceIdType.MESH


def tree_shape(devices):
    chips = devices // 2
    outer = 4 if chips % 4 == 0 else 1
    rest = chips // outer
    middle = 1
    while middle * middle < rest:
        middle *= 2
    return outer, middle, rest // middle


def split(a):
    high = a.astype(jnp.bfloat16)
    low = (a - high.astype(jnp.float32)).astype(jnp.bfloat16)
    return high, low


def mm(a, b):
    dot = functools.partial(jnp.dot, preferred_element_type=jnp.float32)
    return dot(a[0], b[0]) + (dot(a[0], b[1]) + dot(a[1], b[0]))


def eye_mask(size):
    rows = lax.broadcasted_iota(jnp.int32, (size, size), 0)
    cols = lax.broadcasted_iota(jnp.int32, (size, size), 1)
    return rows == cols


def solve(lead_p, lead_n):
    mask = eye_mask(lead_p.shape[0])
    diagonal = jnp.where(mask, lead_p, 0.0)
    inv_rows = 1.0 / jnp.sum(diagonal, axis=1, keepdims=True)
    inv_cols = 1.0 / jnp.sum(diagonal, axis=0, keepdims=True)
    power = jnp.where(mask, 1.0, 0.0) - inv_rows * lead_p
    acc = lead_n
    for index in range(NEWTON):
        power_s = split(power)
        acc = acc + mm(split(acc), power_s)
        if index < NEWTON - 1:
            power = mm(power_s, power_s)
    return acc * inv_cols


def root_less_one(gram):
    mask = eye_mask(gram.shape[0])
    gram_s = split(gram)
    square = mm(gram_s, gram_s)
    inner = jnp.where(mask, 0.375, 0.0) + 0.3125 * gram + 0.2734375 * square
    return 0.5 * gram + mm(split(square), split(inner))


def roots_from(kt):
    c_s = split(kt.T)
    k_s = split(kt)
    s_top = root_less_one(mm(c_s, k_s))
    s_bottom = root_less_one(mm(k_s, c_s))
    return c_s, k_s, split(s_top), split(s_bottom)


def reflect(c_s, s_s, main, other):
    wide = main - mm(c_s, split(other))
    return wide + mm(s_s, split(wide))


def kernel(n, pos_ref, neg_ref, pos_out, neg_out, lead, nb, kbuf, pair, own1,
           bc_send, bc_recv, nb_send, nb_recv, rel_send, ld_send, ld_recv):
    me = lax.axis_index("blk")
    outer, middle, inner = tree_shape(n)
    size = pos_ref.shape[0]
    rows = size // CHUNKS
    core = me % 2
    c = (me // 2) % inner
    b = (me // (2 * inner)) % middle
    a = me // (2 * inner * middle)
    y_step, z_step = 2 * inner, 2 * inner * middle
    even = core == 0
    y_child = even & (c == 0) & (b + 1 < middle)
    y_parent = even & (c == 0) & (b > 0)
    z_child = even & (c == 0) & (b == 0) & (a + 1 < outer)
    z_parent = even & (c == 0) & (b == 0) & (a > 0)
    links = [
        (me >= 1, me - 1), (me + 1 < n, me + 1), (me >= 2, me - 2), (me + 2 < n, me + 2),
        (y_child, me + y_step), (y_parent, me - y_step),
        (z_child, me + z_step), (z_parent, me - z_step),
    ]
    children = [
        (z_child, me + z_step),
        (y_child, me + y_step),
        (even & (c + 1 < inner), me + 2),
        (even & (me > 0), me + 1),
    ]

    barrier = pltpu.get_barrier_semaphore()
    count = jnp.int32(0)
    for there, device in links:
        count = count + jnp.where(there, 1, 0)

        @pl.when(there)
        def _(device=device):
            pl.semaphore_signal(barrier, inc=1, device_id=(device,), device_id_type=MESH)

    pl.semaphore_wait(barrier, count)

    def remote(src, dst, send, recv, device):
        return pltpu.make_async_remote_copy(
            src_ref=src, dst_ref=dst, send_sem=send, recv_sem=recv,
            device_id=(device,), device_id_type=MESH)

    has_next = me + 1 < n
    to_second = even & (me + 2 < n)
    next_copies = [remote(ref, nb.at[i], nb_send.at[i], nb_recv.at[i], me + 1)
                   for i, ref in enumerate((pos_ref, neg_ref))]
    second_copies = [remote(ref, nb.at[2 + i], nb_send.at[2 + i], nb_recv.at[2 + i], me + 2)
                     for i, ref in enumerate((pos_ref, neg_ref))]
    relay_copies = [remote(nb.at[i], nb.at[2 + i], rel_send.at[i], nb_recv.at[2 + i], me + 1)
                    for i in range(2)]
    lead_copies = [remote(ref, lead.at[2 + i], ld_send.at[i], ld_recv.at[i], 0)
                   for i, ref in enumerate((pos_ref, neg_ref))]

    def start(copies):
        for copy in copies:
            copy.start()

    @pl.when(has_next)
    def _():
        start(next_copies)

    @pl.when(me == 1)
    def _():
        start(lead_copies)

    @pl.when(to_second)
    def _():
        start(second_copies)

    def chunk_copy(step, chunk, child, device):
        part = kbuf.at[step, pl.ds(chunk * rows, rows)]
        return remote(part, part, bc_send.at[step, chunk, child], bc_recv.at[step, chunk], device)

    def forward(step, chunk):
        for child, (there, device) in enumerate(children):
            @pl.when(there)
            def _(child=child, device=device):
                chunk_copy(step, chunk, child, device).start()

    def receive(step):
        for chunk in range(CHUNKS):
            chunk_copy(step, chunk, 0, me).wait_recv()
            forward(step, chunk)

    def neighbours():
        @pl.when(me >= 1)
        def _():
            for copy in next_copies:
                copy.wait_recv()

    @pl.when(me < 2)
    def _():
        @pl.when(me == 0)
        def _():
            nb[...] = jnp.zeros_like(nb)
            lead[0] = pos_ref[...]
            lead[1] = neg_ref[...]
            for copy in lead_copies:
                copy.wait_recv()

        @pl.when(me == 1)
        def _():
            for copy in next_copies:
                copy.wait_recv()
            nb[2] = jnp.zeros((size, size), jnp.float32)
            nb[3] = jnp.zeros((size, size), jnp.float32)
            lead[0] = nb[0]
            lead[1] = nb[1]
            lead[2] = pos_ref[...]
            lead[3] = neg_ref[...]

        kbuf[0] = solve(lead[0], lead[1])

        @pl.when(me == 0)
        def _():
            for chunk in range(CHUNKS):
                forward(0, chunk)

    @pl.when(me >= 2)
    def _():
        receive(0)
        for copy in next_copies:
            copy.wait_recv()

        @pl.when(even)
        def _():
            start(relay_copies)

    c_s, k_s, st_s, sb_s = roots_from(kbuf[0])
    for i, pair_part in enumerate((c_s, k_s, st_s, sb_s)):
        pair[i, 0] = pair_part[0]
        pair[i, 1] = pair_part[1]

    def loaded():
        return [(pair[i, 0], pair[i, 1]) for i in range(4)]

    @pl.when(me < 2)
    def _():
        c1, k1, st1, sb1 = loaded()
        lead_p = reflect(c1, st1, lead[0], lead[1])
        lead_n = reflect(k1, sb1, lead[3], lead[2])
        kbuf[1] = solve(lead_p, lead_n)

        @pl.when(me == 0)
        def _():
            for chunk in range(CHUNKS):
                forward(1, chunk)

    @pl.when(me >= 2)
    def _():
        for copy in second_copies:
            copy.wait_recv()

    c1, k1, st1, sb1 = loaded()
    own1[0] = reflect(k1, sb1, neg_ref[...], pos_ref[...])
    own1[1] = reflect(c1, st1, nb[0], nb[1])
    own1[2] = reflect(k1, sb1, nb[1], nb[0])
    own1[3] = reflect(c1, st1, nb[2], nb[3])

    @pl.when(me >= 2)
    def _():
        receive(1)

    c2, k2, st2, sb2 = roots_from(kbuf[1])
    neg_out[...] = reflect(k2, sb2, own1[0], own1[1])
    pos_out[...] = reflect(c2, st2, own1[3], own1[2])

    @pl.when(has_next)
    def _():
        for copy in next_copies:
            copy.wait_send()

    @pl.when(me == 1)
    def _():
        for copy in lead_copies:
            copy.wait_send()

    @pl.when(to_second)
    def _():
        for copy in second_copies:
            copy.wait_send()

    @pl.when(even & (me >= 2))
    def _():
        for copy in relay_copies:
            copy.wait_send()

    for child, (there, device) in enumerate(children):
        @pl.when(there)
        def _(child=child, device=device):
            for step in range(STEPS):
                for chunk in range(CHUNKS):
                    chunk_copy(step, chunk, child, device).wait_send()


def solution(mesh):
    n = mesh.shape["blk"]

    def on_device(positive_row, negative_row):
        size = positive_row.shape[0]
        block = jax.ShapeDtypeStruct((size, size), jnp.float32)
        dma = pltpu.SemaphoreType.DMA
        vmem = pl.BlockSpec(memory_space=pltpu.VMEM)
        return pl.pallas_call(
            functools.partial(kernel, n),
            out_shape=(block, block),
            in_specs=[vmem, vmem],
            out_specs=(vmem, vmem),
            scratch_shapes=[
                pltpu.VMEM((4, size, size), jnp.float32),
                pltpu.VMEM((4, size, size), jnp.float32),
                pltpu.VMEM((STEPS, size, size), jnp.float32),
                pltpu.VMEM((4, 2, size, size), jnp.bfloat16),
                pltpu.VMEM((4, size, size), jnp.float32),
                dma((STEPS, CHUNKS, 4)), dma((STEPS, CHUNKS)),
                dma((4,)), dma((4,)), dma((2,)), dma((2,)), dma((2,)),
            ],
            compiler_params=pltpu.CompilerParams(
                collective_id=0, has_side_effects=True, vmem_limit_bytes=48 * 2**20),
        )(positive_row, negative_row)

    spec = (P(None, "blk"), P(None, "blk"))
    return jax.shard_map(on_device, mesh=mesh, in_specs=spec, out_specs=spec, check_vma=False)
```

```python
import functools

import jax
import jax.numpy as jnp
from jax import lax
from jax.experimental import pallas as pl
from jax.experimental.pallas import tpu as pltpu
from jax.sharding import PartitionSpec as P

STEPS = 2
NEWTON = 4
PIECE = 16
GROUPS = 4
MESH = pl.DeviceIdType.MESH


def split(a):
    high = a.astype(jnp.bfloat16)
    low = (a - high.astype(jnp.float32)).astype(jnp.bfloat16)
    return high, low


def mm(a, b):
    dot = functools.partial(jnp.dot, preferred_element_type=jnp.float32)
    return dot(a[0], b[0]) + (dot(a[0], b[1]) + dot(a[1], b[0]))


def eye_mask(size):
    rows = lax.broadcasted_iota(jnp.int32, (size, size), 0)
    cols = lax.broadcasted_iota(jnp.int32, (size, size), 1)
    return rows == cols


def solve(lead_p, lead_n):
    mask = eye_mask(lead_p.shape[0])
    diagonal = jnp.where(mask, lead_p, 0.0)
    inv_rows = 1.0 / jnp.sum(diagonal, axis=1, keepdims=True)
    inv_cols = 1.0 / jnp.sum(diagonal, axis=0, keepdims=True)
    power = jnp.where(mask, 1.0, 0.0) - inv_rows * lead_p
    acc = lead_n
    for index in range(NEWTON):
        power_s = split(power)
        acc = acc + mm(split(acc), power_s)
        if index < NEWTON - 1:
            power = mm(power_s, power_s)
    return acc * inv_cols


def root_less_one(gram):
    mask = eye_mask(gram.shape[0])
    gram_s = split(gram)
    square = mm(gram_s, gram_s)
    inner = jnp.where(mask, 0.375, 0.0) + 0.3125 * gram + 0.2734375 * square
    return 0.5 * gram + mm(split(square), split(inner))


def roots_from(kt):
    c_s = split(kt.T)
    k_s = split(kt)
    s_top = root_less_one(mm(c_s, k_s))
    s_bottom = root_less_one(mm(k_s, c_s))
    return c_s, k_s, split(s_top), split(s_bottom)


def reflect(c_s, s_s, main, other):
    wide = main - mm(c_s, split(other))
    return wide + mm(s_s, split(wide))


def kernel(n, pos_hbm, neg_hbm, pos_out, neg_out, pos_ref, neg_ref, lead, nb, kbuf, pair, own1,
           in_sem, sc_send, ag_send, bc_recv, core_send, core_recv,
           nb_send, nb_recv, rel_send, ld_send, ld_recv):
    me = lax.axis_index("blk")
    size = pos_ref.shape[0]
    chips = n // 2
    holders = min(chips, size // PIECE)
    rows = size // holders
    per_group = holders // GROUPS
    group_rows = size // GROUPS
    chip = me // 2
    even = me % 2 == 0
    has_next = me + 1 < n
    to_second = even & (me + 2 < n)
    holds = even & (chip < holders)

    loads = [pltpu.make_async_copy(src, dst, in_sem.at[i])
             for i, (src, dst) in enumerate(((pos_hbm, pos_ref), (neg_hbm, neg_ref)))]
    for load in loads:
        load.start()

    barrier = pltpu.get_barrier_semaphore()

    def greet(device):
        pl.semaphore_signal(barrier, inc=1, device_id=(device,), device_id_type=MESH)

    @pl.when(me >= 1)
    def _():
        greet(me - 1)

    @pl.when(has_next)
    def _():
        greet(me + 1)

    @pl.when(even)
    def _():
        def greet_chip(t, carry):
            greet(2 * lax.rem(chip + t, chips))
            return carry

        lax.fori_loop(1, chips, greet_chip, 0)

    count = (jnp.where(me >= 1, 1, 0) + jnp.where(has_next, 1, 0)
             + jnp.where(even, chips - 1, 0))

    @pl.when(me == 0)
    def _():
        for load in loads:
            load.wait()
        kbuf[0] = solve(pos_ref[...], neg_ref[...])
        nb[...] = jnp.zeros_like(nb)

    pl.semaphore_wait(barrier, count)

    def remote(src, dst, send, recv, device):
        return pltpu.make_async_remote_copy(
            src_ref=src, dst_ref=dst, send_sem=send, recv_sem=recv,
            device_id=(device,), device_id_type=MESH)

    hbm = (pos_hbm, neg_hbm)
    next_copies = [remote(hbm[i], nb.at[i], nb_send.at[i], nb_recv.at[i], me + 1) for i in range(2)]
    second_copies = [remote(hbm[i], nb.at[2 + i], nb_send.at[2 + i], nb_recv.at[2 + i], me + 2)
                     for i in range(2)]
    relay_copies = [remote(nb.at[i], nb.at[2 + i], rel_send.at[i], nb_recv.at[2 + i], me + 1)
                    for i in range(2)]
    lead_copies = [remote(hbm[i], lead.at[i], ld_send.at[i], ld_recv.at[i], 0) for i in range(2)]

    def start(copies):
        for copy in copies:
            copy.start()

    def piece_of(step, piece):
        return kbuf.at[step, pl.ds(pl.multiple_of(piece * rows, rows), rows)]

    def scatter_copy(step, piece):
        part = piece_of(step, piece)
        return remote(part, part, sc_send.at[step, piece], bc_recv.at[step, piece], 2 * piece)

    def gather_copy(step, target):
        part = piece_of(step, chip)
        return remote(part, part, ag_send.at[step, target], bc_recv.at[step, chip], 2 * target)

    def core_copy(step, group):
        part = kbuf.at[step, pl.ds(group * group_rows, group_rows)]
        return remote(part, part, core_send.at[step, group], core_recv.at[step, group], me + 1)

    def each_target(step, act):
        def one(t, carry):
            target = lax.rem(chip + t, chips)

            @pl.when(target != 0)
            def _():
                act(gather_copy(step, target))

            return carry

        lax.fori_loop(1, chips, one, 0)

    def each_scatter(step, act):
        def one(t, carry):
            act(scatter_copy(step, t))
            return carry

        lax.fori_loop(1, holders, one, 0)

    def publish(step):
        each_scatter(step, lambda copy: copy.start())
        each_target(step, lambda copy: copy.start())
        for group in range(GROUPS):
            core_copy(step, group).start()

    def receive(step):
        @pl.when(holds)
        def _():
            scatter_copy(step, chip).wait_recv()
            each_target(step, lambda copy: copy.start())

        @pl.when(even)
        def _():
            for group in range(GROUPS):
                for piece in range(group * per_group, (group + 1) * per_group):
                    @pl.when(chip != piece)
                    def _(piece=piece):
                        scatter_copy(step, piece).wait_recv()

                core_copy(step, group).start()

        @pl.when(jnp.logical_not(even))
        def _():
            for group in range(GROUPS):
                core_copy(step, group).wait_recv()

    @pl.when(me == 0)
    def _():
        publish(0)

    @pl.when(me == 1)
    def _():
        start(lead_copies)

    @pl.when(has_next)
    def _():
        start(next_copies)

    @pl.when(to_second)
    def _():
        start(second_copies)

    @pl.when(me >= 1)
    def _():
        for load in loads:
            load.wait()
        receive(0)
        for copy in next_copies:
            copy.wait_recv()

    @pl.when(even & (me >= 2))
    def _():
        start(relay_copies)

    @pl.when(me == 1)
    def _():
        nb[2] = jnp.zeros((size, size), jnp.float32)
        nb[3] = jnp.zeros((size, size), jnp.float32)

    for i, pair_part in enumerate(roots_from(kbuf[0])):
        pair[i, 0] = pair_part[0]
        pair[i, 1] = pair_part[1]

    def loaded():
        return [(pair[i, 0], pair[i, 1]) for i in range(4)]

    @pl.when(me == 0)
    def _():
        c1, k1, st1, sb1 = loaded()
        for copy in lead_copies:
            copy.wait_recv()
        lead_p = reflect(c1, st1, pos_ref[...], neg_ref[...])
        lead_n = reflect(k1, sb1, lead[1], lead[0])
        kbuf[1] = solve(lead_p, lead_n)
        publish(1)

    @pl.when(me >= 2)
    def _():
        for copy in second_copies:
            copy.wait_recv()

    c1, k1, st1, sb1 = loaded()
    own1[0] = reflect(k1, sb1, neg_ref[...], pos_ref[...])
    own1[1] = reflect(c1, st1, nb[0], nb[1])
    own1[2] = reflect(k1, sb1, nb[1], nb[0])
    own1[3] = reflect(c1, st1, nb[2], nb[3])

    @pl.when(me >= 1)
    def _():
        receive(1)

    c2, k2, st2, sb2 = roots_from(kbuf[1])
    neg_out[...] = reflect(k2, sb2, own1[0], own1[1])
    pos_out[...] = reflect(c2, st2, own1[3], own1[2])

    def sent(copies):
        for copy in copies:
            copy.wait_send()

    @pl.when(has_next)
    def _():
        sent(next_copies)

    @pl.when(me == 1)
    def _():
        sent(lead_copies)

    @pl.when(to_second)
    def _():
        sent(second_copies)

    @pl.when(even & (me >= 2))
    def _():
        sent(relay_copies)

    for step in range(STEPS):
        @pl.when(me == 0)
        def _(step=step):
            each_scatter(step, lambda copy: copy.wait_send())

        @pl.when(holds)
        def _(step=step):
            each_target(step, lambda copy: copy.wait_send())

        @pl.when(even)
        def _(step=step):
            for group in range(GROUPS):
                core_copy(step, group).wait_send()


def solution(mesh):
    n = mesh.shape["blk"]

    def on_device(positive_row, negative_row):
        size = positive_row.shape[0]
        block = jax.ShapeDtypeStruct((size, size), jnp.float32)
        chips = n // 2
        holders = min(chips, size // PIECE)
        dma = pltpu.SemaphoreType.DMA
        vmem = pl.BlockSpec(memory_space=pltpu.VMEM)
        hbm = pl.BlockSpec(memory_space=pltpu.HBM)
        return pl.pallas_call(
            functools.partial(kernel, n),
            out_shape=(block, block),
            in_specs=[hbm, hbm],
            out_specs=(vmem, vmem),
            scratch_shapes=[
                pltpu.VMEM((size, size), jnp.float32),
                pltpu.VMEM((size, size), jnp.float32),
                pltpu.VMEM((2, size, size), jnp.float32),
                pltpu.VMEM((4, size, size), jnp.float32),
                pltpu.VMEM((STEPS, size, size), jnp.float32),
                pltpu.VMEM((4, 2, size, size), jnp.bfloat16),
                pltpu.VMEM((4, size, size), jnp.float32),
                dma((2,)), dma((STEPS, holders)), dma((STEPS, chips)), dma((STEPS, holders)),
                dma((STEPS, GROUPS)), dma((STEPS, GROUPS)),
                dma((4,)), dma((4,)), dma((2,)), dma((2,)), dma((2,)),
            ],
            compiler_params=pltpu.CompilerParams(
                collective_id=0, has_side_effects=True, vmem_limit_bytes=64 * 2**20),
        )(positive_row, negative_row)

    spec = (P(None, "blk"), P(None, "blk"))
    return jax.shard_map(on_device, mesh=mesh, in_specs=spec, out_specs=spec, check_vma=False)
```

```python
import functools

import jax
import jax.numpy as jnp
from jax import lax
from jax.experimental import pallas as pl
from jax.experimental.pallas import tpu as pltpu
from jax.sharding import PartitionSpec as P

STEPS = 2
NEWTON = 4
PIECE = 16
GROUPS = 4
MESH = pl.DeviceIdType.MESH


def split(a):
    high = a.astype(jnp.bfloat16)
    low = (a - high.astype(jnp.float32)).astype(jnp.bfloat16)
    return high, low


def mm(a, b):
    dot = functools.partial(jnp.dot, preferred_element_type=jnp.float32)
    return dot(a[0], b[0]) + (dot(a[0], b[1]) + dot(a[1], b[0]))


def eye_mask(size):
    rows = lax.broadcasted_iota(jnp.int32, (size, size), 0)
    cols = lax.broadcasted_iota(jnp.int32, (size, size), 1)
    return rows == cols


def solve(lead_p, lead_n):
    mask = eye_mask(lead_p.shape[0])
    diagonal = jnp.where(mask, lead_p, 0.0)
    inv_rows = 1.0 / jnp.sum(diagonal, axis=1, keepdims=True)
    inv_cols = 1.0 / jnp.sum(diagonal, axis=0, keepdims=True)
    power = jnp.where(mask, 1.0, 0.0) - inv_rows * lead_p
    acc = lead_n
    for index in range(NEWTON):
        power_s = split(power)
        acc = acc + mm(split(acc), power_s)
        if index < NEWTON - 1:
            power = mm(power_s, power_s)
    return acc * inv_cols


def root_less_one(gram):
    mask = eye_mask(gram.shape[0])
    gram_s = split(gram)
    square = mm(gram_s, gram_s)
    inner = jnp.where(mask, 0.375, 0.0) + 0.3125 * gram + 0.2734375 * square
    return 0.5 * gram + mm(split(square), split(inner))


def roots_from(kt):
    c_s = split(kt.T)
    k_s = split(kt)
    s_top = root_less_one(mm(c_s, k_s))
    s_bottom = root_less_one(mm(k_s, c_s))
    return c_s, k_s, split(s_top), split(s_bottom)


def reflect(c_s, s_s, main, other):
    wide = main - mm(c_s, split(other))
    return wide + mm(s_s, split(wide))


def kernel(n, pos_hbm, neg_hbm, pos_out, neg_out, pos_ref, neg_ref, lead, nb, kbuf, pair, own1,
           in_sem, sc_send, ag_send, bc_recv, core_send, core_recv,
           nb_send, nb_recv, sh_send, sh_recv, ld_send, ld_recv):
    me = lax.axis_index("blk")
    size = pos_ref.shape[0]
    chips = n // 2
    holders = min(chips, size // PIECE)
    rows = size // holders
    per_group = holders // GROUPS
    group_rows = size // GROUPS
    chip = me // 2
    even = me % 2 == 0
    has_next = me + 1 < n
    holds = even & (chip < holders)

    loads = [pltpu.make_async_copy(src, dst, in_sem.at[i])
             for i, (src, dst) in enumerate(((pos_hbm, pos_ref), (neg_hbm, neg_ref)))]
    for load in loads:
        load.start()

    barrier = pltpu.get_barrier_semaphore()

    def greet(device):
        pl.semaphore_signal(barrier, inc=1, device_id=(device,), device_id_type=MESH)

    @pl.when(me >= 1)
    def _():
        greet(me - 1)

    @pl.when(has_next)
    def _():
        greet(me + 1)

    @pl.when(even)
    def _():
        def greet_chip(t, carry):
            greet(2 * lax.rem(chip + t, chips))
            return carry

        lax.fori_loop(1, chips, greet_chip, 0)

    count = (jnp.where(me >= 1, 1, 0) + jnp.where(has_next, 1, 0)
             + jnp.where(even, chips - 1, 0))

    @pl.when(me == 0)
    def _():
        for load in loads:
            load.wait()
        kbuf[0] = solve(pos_ref[...], neg_ref[...])
        nb[...] = jnp.zeros_like(nb)

    pl.semaphore_wait(barrier, count)

    def remote(src, dst, send, recv, device):
        return pltpu.make_async_remote_copy(
            src_ref=src, dst_ref=dst, send_sem=send, recv_sem=recv,
            device_id=(device,), device_id_type=MESH)

    hbm = (pos_hbm, neg_hbm)
    next_copies = [remote(hbm[i], nb.at[i], nb_send.at[i], nb_recv.at[i], me + 1) for i in range(2)]
    shift_copy = remote(own1.at[1], own1.at[3], sh_send, sh_recv, me + 1)
    lead_copies = [remote(hbm[i], lead.at[i], ld_send.at[i], ld_recv.at[i], 0) for i in range(2)]

    def start(copies):
        for copy in copies:
            copy.start()

    def piece_of(step, piece):
        return kbuf.at[step, pl.ds(pl.multiple_of(piece * rows, rows), rows)]

    def scatter_copy(step, piece):
        part = piece_of(step, piece)
        return remote(part, part, sc_send.at[step, piece], bc_recv.at[step, piece], 2 * piece)

    def gather_copy(step, target):
        part = piece_of(step, chip)
        return remote(part, part, ag_send.at[step, target], bc_recv.at[step, chip], 2 * target)

    def core_copy(step, group):
        part = kbuf.at[step, pl.ds(group * group_rows, group_rows)]
        return remote(part, part, core_send.at[step, group], core_recv.at[step, group], me + 1)

    def each_target(step, act):
        def one(t, carry):
            target = lax.rem(chip + t, chips)

            @pl.when(target != 0)
            def _():
                act(gather_copy(step, target))

            return carry

        lax.fori_loop(1, chips, one, 0)

    def each_scatter(step, act):
        def one(t, carry):
            act(scatter_copy(step, t))
            return carry

        lax.fori_loop(1, holders, one, 0)

    def publish(step):
        each_scatter(step, lambda copy: copy.start())
        each_target(step, lambda copy: copy.start())
        for group in range(GROUPS):
            core_copy(step, group).start()

    def receive(step):
        @pl.when(holds)
        def _():
            scatter_copy(step, chip).wait_recv()
            each_target(step, lambda copy: copy.start())

        @pl.when(even)
        def _():
            for group in range(GROUPS):
                for piece in range(group * per_group, (group + 1) * per_group):
                    @pl.when(chip != piece)
                    def _(piece=piece):
                        scatter_copy(step, piece).wait_recv()

                core_copy(step, group).start()

        @pl.when(jnp.logical_not(even))
        def _():
            for group in range(GROUPS):
                core_copy(step, group).wait_recv()

    @pl.when(me == 0)
    def _():
        publish(0)

    @pl.when(me == 1)
    def _():
        start(lead_copies)

    @pl.when(has_next)
    def _():
        start(next_copies)

    @pl.when(me >= 1)
    def _():
        for load in loads:
            load.wait()
        receive(0)
        for copy in next_copies:
            copy.wait_recv()

    for i, pair_part in enumerate(roots_from(kbuf[0])):
        pair[i, 0] = pair_part[0]
        pair[i, 1] = pair_part[1]

    def loaded():
        return [(pair[i, 0], pair[i, 1]) for i in range(4)]

    @pl.when(me == 0)
    def _():
        c1, k1, st1, sb1 = loaded()
        for copy in lead_copies:
            copy.wait_recv()
        lead_p = reflect(c1, st1, pos_ref[...], neg_ref[...])
        lead_n = reflect(k1, sb1, lead[1], lead[0])
        kbuf[1] = solve(lead_p, lead_n)
        publish(1)

    c1, k1, st1, sb1 = loaded()
    own1[1] = reflect(c1, st1, nb[0], nb[1])

    @pl.when(has_next)
    def _():
        shift_copy.start()

    own1[0] = reflect(k1, sb1, neg_ref[...], pos_ref[...])
    own1[2] = reflect(k1, sb1, nb[1], nb[0])

    @pl.when(me >= 1)
    def _():
        receive(1)
        shift_copy.wait_recv()

    @pl.when(me == 0)
    def _():
        own1[3] = jnp.zeros((size, size), jnp.float32)

    c2, k2, st2, sb2 = roots_from(kbuf[1])
    neg_out[...] = reflect(k2, sb2, own1[0], own1[1])
    pos_out[...] = reflect(c2, st2, own1[3], own1[2])

    def sent(copies):
        for copy in copies:
            copy.wait_send()

    @pl.when(has_next)
    def _():
        sent(next_copies + [shift_copy])

    @pl.when(me == 1)
    def _():
        sent(lead_copies)

    for step in range(STEPS):
        @pl.when(me == 0)
        def _(step=step):
            each_scatter(step, lambda copy: copy.wait_send())

        @pl.when(holds)
        def _(step=step):
            each_target(step, lambda copy: copy.wait_send())

        @pl.when(even)
        def _(step=step):
            for group in range(GROUPS):
                core_copy(step, group).wait_send()


def solution(mesh):
    n = mesh.shape["blk"]

    def on_device(positive_row, negative_row):
        size = positive_row.shape[0]
        chips = n // 2
        holders = min(chips, size // PIECE)
        dma = pltpu.SemaphoreType.DMA
        vmem = pl.BlockSpec(memory_space=pltpu.VMEM)
        hbm = pl.BlockSpec(memory_space=pltpu.HBM)
        return pl.pallas_call(
            functools.partial(kernel, n),
            out_shape=(pltpu.VMEM((size, size), jnp.float32),) * 2,
            in_specs=[hbm, hbm],
            out_specs=(vmem, vmem),
            scratch_shapes=[
                pltpu.VMEM((size, size), jnp.float32),
                pltpu.VMEM((size, size), jnp.float32),
                pltpu.VMEM((2, size, size), jnp.float32),
                pltpu.VMEM((2, size, size), jnp.float32),
                pltpu.VMEM((STEPS, size, size), jnp.float32),
                pltpu.VMEM((4, 2, size, size), jnp.bfloat16),
                pltpu.VMEM((4, size, size), jnp.float32),
                dma((2,)), dma((STEPS, holders)), dma((STEPS, chips)), dma((STEPS, holders)),
                dma((STEPS, GROUPS)), dma((STEPS, GROUPS)),
                dma((2,)), dma((2,)), dma, dma, dma((2,)), dma((2,)),
            ],
            compiler_params=pltpu.CompilerParams(
                collective_id=0, has_side_effects=True, vmem_limit_bytes=64000000),
        )(positive_row, negative_row)

    spec = (P(None, "blk"), P(None, "blk"))
    return jax.shard_map(on_device, mesh=mesh, in_specs=spec, out_specs=spec, check_vma=False)
```

```python
import functools

import jax
import jax.numpy as jnp
from jax import lax
from jax.experimental import pallas as pl
from jax.experimental.pallas import tpu as pltpu
from jax.sharding import PartitionSpec as P

STEPS = 2
NEWTON = 4
PIECE = 16
GROUPS = 4
MESH = pl.DeviceIdType.MESH


def split(a):
    high = a.astype(jnp.bfloat16)
    low = (a - high.astype(jnp.float32)).astype(jnp.bfloat16)
    return high, low


def mm(a, b):
    dot = functools.partial(jnp.dot, preferred_element_type=jnp.float32)
    return dot(a[0], b[0]) + (dot(a[0], b[1]) + dot(a[1], b[0]))


def eye_mask(size):
    rows = lax.broadcasted_iota(jnp.int32, (size, size), 0)
    cols = lax.broadcasted_iota(jnp.int32, (size, size), 1)
    return rows == cols


def solve(lead_p, lead_n):
    mask = eye_mask(lead_p.shape[0])
    diagonal = jnp.where(mask, lead_p, 0.0)
    inv_rows = 1.0 / jnp.sum(diagonal, axis=1, keepdims=True)
    inv_cols = 1.0 / jnp.sum(diagonal, axis=0, keepdims=True)
    power = jnp.where(mask, 1.0, 0.0) - inv_rows * lead_p
    acc = lead_n
    for index in range(NEWTON):
        power_s = split(power)
        acc = acc + mm(split(acc), power_s)
        if index < NEWTON - 1:
            power = mm(power_s, power_s)
    return acc * inv_cols


def root_less_one(gram):
    mask = eye_mask(gram.shape[0])
    gram_s = split(gram)
    square = mm(gram_s, gram_s)
    inner = jnp.where(mask, 0.375, 0.0) + 0.3125 * gram + 0.2734375 * square
    return 0.5 * gram + mm(split(square), split(inner))


def roots_from(kt):
    c_s = split(kt.T)
    k_s = split(kt)
    s_top = root_less_one(mm(c_s, k_s))
    s_bottom = root_less_one(mm(k_s, c_s))
    return c_s, k_s, split(s_top), split(s_bottom)


def reflect(c_s, s_s, main, other):
    wide = main - mm(c_s, split(other))
    return wide + mm(s_s, split(wide))


def kernel(n, pos_hbm, neg_hbm, pos_out, neg_out, pos_ref, neg_ref, lead, nb, kbuf, pair, own1,
           in_sem, sc_send, ag_send, bc_recv, core_send, core_recv,
           nb_send, nb_recv, sh_send, sh_recv, ld_send, ld_recv):
    me = lax.axis_index("blk")
    size = pos_ref.shape[0]
    chips = n // 2
    holders = min(chips, size // PIECE)
    rows = size // holders
    per_group = holders // GROUPS
    group_rows = size // GROUPS
    chip = me // 2
    even = me % 2 == 0
    has_next = me + 1 < n
    relays = even & (me > 0)
    holds = (relays & (chip < holders)) | (me == 1)

    loads = [pltpu.make_async_copy(src, dst, in_sem.at[i])
             for i, (src, dst) in enumerate(((pos_hbm, pos_ref), (neg_hbm, neg_ref)))]
    for load in loads:
        load.start()

    barrier = pltpu.get_barrier_semaphore()

    def greet(device):
        pl.semaphore_signal(barrier, inc=1, device_id=(device,), device_id_type=MESH)

    @pl.when(me >= 1)
    def _():
        greet(me - 1)

    @pl.when(has_next)
    def _():
        greet(me + 1)

    @pl.when(even)
    def _():
        def greet_chip(t, carry):
            greet(2 * lax.rem(chip + t, chips))
            return carry

        lax.fori_loop(1, chips, greet_chip, 0)

    @pl.when(me == 1)
    def _():
        def greet_even(t, carry):
            greet(2 * t)
            return carry

        lax.fori_loop(2, chips, greet_even, 0)

    @pl.when(even & (chip >= 2))
    def _():
        greet(1)

    count = (jnp.where(me >= 1, 1, 0) + jnp.where(has_next, 1, 0)
             + jnp.where(even, chips - 1, 0) + jnp.where(me == 1, chips - 2, 0)
             + jnp.where(even & (chip >= 2), 1, 0))

    @pl.when(me == 0)
    def _():
        for load in loads:
            load.wait()
        kbuf[0] = solve(pos_ref[...], neg_ref[...])
        nb[...] = jnp.zeros_like(nb)

    pl.semaphore_wait(barrier, count)

    def remote(src, dst, send, recv, device):
        return pltpu.make_async_remote_copy(
            src_ref=src, dst_ref=dst, send_sem=send, recv_sem=recv,
            device_id=(device,), device_id_type=MESH)

    hbm = (pos_hbm, neg_hbm)
    next_copies = [remote(hbm[i], nb.at[i], nb_send.at[i], nb_recv.at[i], me + 1) for i in range(2)]
    shift_copy = remote(own1.at[1], own1.at[3], sh_send, sh_recv, me + 1)
    lead_copies = [remote(hbm[i], lead.at[i], ld_send.at[i], ld_recv.at[i], 0) for i in range(2)]

    def start(copies):
        for copy in copies:
            copy.start()

    def piece_of(step, piece):
        return kbuf.at[step, pl.ds(pl.multiple_of(piece * rows, rows), rows)]

    def scatter_copy(step, piece):
        part = piece_of(step, piece)
        return remote(part, part, sc_send.at[step, piece], bc_recv.at[step, piece], 2 * piece)

    def gather_copy(step, target):
        part = piece_of(step, chip)
        return remote(part, part, ag_send.at[step, target], bc_recv.at[step, chip], 2 * target)

    def core_copy(step, group):
        part = kbuf.at[step, pl.ds(group * group_rows, group_rows)]
        return remote(part, part, core_send.at[step, group], core_recv.at[step, group], me + 1)

    def each_target(step, act):
        def one(t, carry):
            target = lax.rem(chip + t, chips)

            @pl.when(target != 0)
            def _():
                act(gather_copy(step, target))

            return carry

        lax.fori_loop(1, chips, one, 0)

    def each_scatter(step, act):
        def one(t, carry):
            act(scatter_copy(step, t))
            return carry

        lax.fori_loop(1, holders, one, 0)

    def publish(step):
        core_copy(step, 0).start()
        each_scatter(step, lambda copy: copy.start())
        for group in range(1, GROUPS):
            core_copy(step, group).start()

    def receive(step):
        @pl.when(holds & even)
        def _():
            scatter_copy(step, chip).wait_recv()
            each_target(step, lambda copy: copy.start())

        @pl.when(even)
        def _():
            for group in range(GROUPS):
                for piece in range(group * per_group, (group + 1) * per_group):
                    @pl.when(chip != piece)
                    def _(piece=piece):
                        scatter_copy(step, piece).wait_recv()

                core_copy(step, group).start()

        @pl.when(jnp.logical_not(even))
        def _():
            for group in range(GROUPS):
                core_copy(step, group).wait_recv()
                if group == 0:
                    @pl.when(me == 1)
                    def _():
                        each_target(step, lambda copy: copy.start())

    @pl.when(me == 0)
    def _():
        publish(0)

    @pl.when(me == 1)
    def _():
        start(lead_copies)

    @pl.when(has_next)
    def _():
        start(next_copies)

    @pl.when(me >= 1)
    def _():
        for load in loads:
            load.wait()
        receive(0)
        for copy in next_copies:
            copy.wait_recv()

    for i, pair_part in enumerate(roots_from(kbuf[0])):
        pair[i, 0] = pair_part[0]
        pair[i, 1] = pair_part[1]

    def loaded():
        return [(pair[i, 0], pair[i, 1]) for i in range(4)]

    @pl.when(me == 0)
    def _():
        c1, k1, st1, sb1 = loaded()
        for copy in lead_copies:
            copy.wait_recv()
        lead_p = reflect(c1, st1, pos_ref[...], neg_ref[...])
        lead_n = reflect(k1, sb1, lead[1], lead[0])
        kbuf[1] = solve(lead_p, lead_n)
        publish(1)

    c1, k1, st1, sb1 = loaded()
    own1[1] = reflect(c1, st1, nb[0], nb[1])

    @pl.when(has_next)
    def _():
        shift_copy.start()

    own1[0] = reflect(k1, sb1, neg_ref[...], pos_ref[...])
    own1[2] = reflect(k1, sb1, nb[1], nb[0])

    @pl.when(me >= 1)
    def _():
        receive(1)
        shift_copy.wait_recv()

    @pl.when(me == 0)
    def _():
        own1[3] = jnp.zeros((size, size), jnp.float32)

    c2, k2, st2, sb2 = roots_from(kbuf[1])
    neg_out[...] = reflect(k2, sb2, own1[0], own1[1])
    pos_out[...] = reflect(c2, st2, own1[3], own1[2])

    def sent(copies):
        for copy in copies:
            copy.wait_send()

    @pl.when(has_next)
    def _():
        sent(next_copies + [shift_copy])

    @pl.when(me == 1)
    def _():
        sent(lead_copies)

    for step in range(STEPS):
        @pl.when(me == 0)
        def _(step=step):
            each_scatter(step, lambda copy: copy.wait_send())

        @pl.when(holds)
        def _(step=step):
            each_target(step, lambda copy: copy.wait_send())

        @pl.when(even)
        def _(step=step):
            for group in range(GROUPS):
                core_copy(step, group).wait_send()


def solution(mesh):
    n = mesh.shape["blk"]

    def on_device(positive_row, negative_row):
        size = positive_row.shape[0]
        chips = n // 2
        holders = min(chips, size // PIECE)
        dma = pltpu.SemaphoreType.DMA
        vmem = pl.BlockSpec(memory_space=pltpu.VMEM)
        hbm = pl.BlockSpec(memory_space=pltpu.HBM)
        return pl.pallas_call(
            functools.partial(kernel, n),
            out_shape=(pltpu.VMEM((size, size), jnp.float32),) * 2,
            in_specs=[hbm, hbm],
            out_specs=(vmem, vmem),
            scratch_shapes=[
                pltpu.VMEM((size, size), jnp.float32),
                pltpu.VMEM((size, size), jnp.float32),
                pltpu.VMEM((2, size, size), jnp.float32),
                pltpu.VMEM((2, size, size), jnp.float32),
                pltpu.VMEM((STEPS, size, size), jnp.float32),
                pltpu.VMEM((4, 2, size, size), jnp.bfloat16),
                pltpu.VMEM((4, size, size), jnp.float32),
                dma((2,)), dma((STEPS, holders)), dma((STEPS, chips)), dma((STEPS, holders)),
                dma((STEPS, GROUPS)), dma((STEPS, GROUPS)),
                dma((2,)), dma((2,)), dma, dma, dma((2,)), dma((2,)),
            ],
            compiler_params=pltpu.CompilerParams(
                collective_id=0, has_side_effects=True, vmem_limit_bytes=64000000),
        )(positive_row, negative_row)

    spec = (P(None, "blk"), P(None, "blk"))
    return jax.shard_map(on_device, mesh=mesh, in_specs=spec, out_specs=spec, check_vma=False)
```

```python
import functools

import jax
import jax.numpy as jnp
from jax import lax
from jax.experimental import pallas as pl
from jax.experimental.pallas import tpu as pltpu
from jax.sharding import PartitionSpec as P

STEPS = 2
NEWTON = 4
PIECE = 16
GROUPS = 4
MESH = pl.DeviceIdType.MESH


def repeat(first, last, body):
    if last - first <= 32:
        for t in range(first, last):
            body(t)
    else:
        def one(t, carry):
            body(t)
            return carry

        lax.fori_loop(first, last, one, 0)


def split(a):
    high = a.astype(jnp.bfloat16)
    low = (a - high.astype(jnp.float32)).astype(jnp.bfloat16)
    return high, low


def mm(a, b):
    dot = functools.partial(jnp.dot, preferred_element_type=jnp.float32)
    return dot(a[0], b[0]) + (dot(a[0], b[1]) + dot(a[1], b[0]))


def eye_mask(size):
    rows = lax.broadcasted_iota(jnp.int32, (size, size), 0)
    cols = lax.broadcasted_iota(jnp.int32, (size, size), 1)
    return rows == cols


def solve(lead_p, lead_n):
    mask = eye_mask(lead_p.shape[0])
    diagonal = jnp.where(mask, lead_p, 0.0)
    inv_rows = 1.0 / jnp.sum(diagonal, axis=1, keepdims=True)
    inv_cols = 1.0 / jnp.sum(diagonal, axis=0, keepdims=True)
    power = jnp.where(mask, 1.0, 0.0) - inv_rows * lead_p
    acc = lead_n
    for index in range(NEWTON):
        power_s = split(power)
        acc = acc + mm(split(acc), power_s)
        if index < NEWTON - 1:
            power = mm(power_s, power_s)
    return acc * inv_cols


def root_less_one(gram):
    mask = eye_mask(gram.shape[0])
    gram_s = split(gram)
    square = mm(gram_s, gram_s)
    inner = jnp.where(mask, 0.375, 0.0) + 0.3125 * gram + 0.2734375 * square
    return 0.5 * gram + mm(split(square), split(inner))


def roots_from(kt):
    c_s = split(kt.T)
    k_s = split(kt)
    s_top = root_less_one(mm(c_s, k_s))
    s_bottom = root_less_one(mm(k_s, c_s))
    return c_s, k_s, split(s_top), split(s_bottom)


def reflect(c_s, s_s, main, other):
    wide = main - mm(c_s, split(other))
    return wide + mm(s_s, split(wide))


def kernel(n, pos_hbm, neg_hbm, pos_out, neg_out, pos_ref, neg_ref, lead, nb, kbuf, pair, own1,
           in_sem, sc_send, ag_send, bc_recv, core_send, core_recv,
           nb_send, nb_recv, sh_send, sh_recv, ld_send, ld_recv):
    me = lax.axis_index("blk")
    size = pos_ref.shape[0]
    chips = n // 2
    holders = min(chips, size // PIECE)
    rows = size // holders
    per_group = holders // GROUPS
    group_rows = size // GROUPS
    chip = me // 2
    even = me % 2 == 0
    has_next = me + 1 < n
    holds = even & (chip < holders)

    loads = [pltpu.make_async_copy(src, dst, in_sem.at[i])
             for i, (src, dst) in enumerate(((pos_hbm, pos_ref), (neg_hbm, neg_ref)))]
    for load in loads:
        load.start()

    barrier = pltpu.get_barrier_semaphore()

    def greet(device):
        pl.semaphore_signal(barrier, inc=1, device_id=(device,), device_id_type=MESH)

    @pl.when(me >= 1)
    def _():
        greet(me - 1)

    @pl.when(has_next)
    def _():
        greet(me + 1)

    @pl.when(even)
    def _():
        def greet_chip(t, carry):
            greet(2 * lax.rem(chip + t, chips))
            return carry

        lax.fori_loop(1, chips, greet_chip, 0)

    count = (jnp.where(me >= 1, 1, 0) + jnp.where(has_next, 1, 0)
             + jnp.where(even, chips - 1, 0))

    @pl.when(me == 0)
    def _():
        for load in loads:
            load.wait()
        kbuf[0] = solve(pos_ref[...], neg_ref[...])
        nb[...] = jnp.zeros_like(nb)

    pl.semaphore_wait(barrier, count)

    def remote(src, dst, send, recv, device):
        return pltpu.make_async_remote_copy(
            src_ref=src, dst_ref=dst, send_sem=send, recv_sem=recv,
            device_id=(device,), device_id_type=MESH)

    hbm = (pos_hbm, neg_hbm)
    next_copies = [remote(hbm[i], nb.at[i], nb_send.at[i], nb_recv.at[i], me + 1) for i in range(2)]
    shift_copy = remote(own1.at[1], own1.at[3], sh_send, sh_recv, me + 1)
    lead_copies = [remote(hbm[i], lead.at[i], ld_send.at[i], ld_recv.at[i], 0) for i in range(2)]

    def start(copies):
        for copy in copies:
            copy.start()

    def piece_of(step, piece):
        return kbuf.at[step, pl.ds(pl.multiple_of(piece * rows, rows), rows)]

    def scatter_copy(step, piece):
        part = kbuf.at[step, pl.ds(piece * rows if isinstance(piece, int)
                                   else pl.multiple_of(piece * rows, rows), rows)]
        return remote(part, part, sc_send.at[step, piece], bc_recv.at[step, piece], 2 * piece)

    def gather_copy(step, target):
        part = piece_of(step, chip)
        return remote(part, part, ag_send.at[step, target], bc_recv.at[step, chip], 2 * target)

    def root_copy(step, target):
        part = kbuf.at[step, pl.ds(0, rows)]
        return remote(part, part, ag_send.at[step, target], bc_recv.at[step, 0], 2 * target)

    def core_copy(step, group):
        part = kbuf.at[step, pl.ds(group * group_rows, group_rows)]
        return remote(part, part, core_send.at[step, group], core_recv.at[step, group], me + 1)

    def each_target(step, act):
        def one(t):
            target = lax.rem(chip + t, chips)

            @pl.when(target != 0)
            def _():
                act(gather_copy(step, target))

        repeat(1, chips, one)

    def each_scatter(step, act):
        repeat(1, holders, lambda t: act(scatter_copy(step, t)))

    def publish(step):
        each_scatter(step, lambda copy: copy.start())
        repeat(1, chips, lambda t: root_copy(step, t).start())
        for group in range(GROUPS):
            core_copy(step, group).start()

    def receive(step):
        @pl.when(holds)
        def _():
            scatter_copy(step, chip).wait_recv()
            each_target(step, lambda copy: copy.start())

        @pl.when(even)
        def _():
            for group in range(GROUPS):
                for piece in range(group * per_group, (group + 1) * per_group):
                    @pl.when(chip != piece)
                    def _(piece=piece):
                        scatter_copy(step, piece).wait_recv()

                core_copy(step, group).start()

        @pl.when(jnp.logical_not(even))
        def _():
            for group in range(GROUPS):
                core_copy(step, group).wait_recv()

    @pl.when(me == 0)
    def _():
        publish(0)

    @pl.when(me == 1)
    def _():
        start(lead_copies)

    @pl.when(has_next)
    def _():
        start(next_copies)

    @pl.when(me >= 1)
    def _():
        for load in loads:
            load.wait()
        receive(0)
        for copy in next_copies:
            copy.wait_recv()

    for i, pair_part in enumerate(roots_from(kbuf[0])):
        pair[i, 0] = pair_part[0]
        pair[i, 1] = pair_part[1]

    def loaded():
        return [(pair[i, 0], pair[i, 1]) for i in range(4)]

    @pl.when(me == 0)
    def _():
        c1, k1, st1, sb1 = loaded()
        for copy in lead_copies:
            copy.wait_recv()
        lead_p = reflect(c1, st1, pos_ref[...], neg_ref[...])
        lead_n = reflect(k1, sb1, lead[1], lead[0])
        kbuf[1] = solve(lead_p, lead_n)
        publish(1)

    c1, k1, st1, sb1 = loaded()
    own1[1] = reflect(c1, st1, nb[0], nb[1])

    @pl.when(has_next)
    def _():
        shift_copy.start()

    own1[0] = reflect(k1, sb1, neg_ref[...], pos_ref[...])
    own1[2] = reflect(k1, sb1, nb[1], nb[0])

    @pl.when(me >= 1)
    def _():
        receive(1)
        shift_copy.wait_recv()

    @pl.when(me == 0)
    def _():
        own1[3] = jnp.zeros((size, size), jnp.float32)

    c2, k2, st2, sb2 = roots_from(kbuf[1])
    neg_out[...] = reflect(k2, sb2, own1[0], own1[1])
    pos_out[...] = reflect(c2, st2, own1[3], own1[2])

    def sent(copies):
        for copy in copies:
            copy.wait_send()

    @pl.when(has_next)
    def _():
        sent(next_copies + [shift_copy])

    @pl.when(me == 1)
    def _():
        sent(lead_copies)

    for step in range(STEPS):
        @pl.when(me == 0)
        def _(step=step):
            each_scatter(step, lambda copy: copy.wait_send())

        @pl.when(holds)
        def _(step=step):
            each_target(step, lambda copy: copy.wait_send())

        @pl.when(even)
        def _(step=step):
            for group in range(GROUPS):
                core_copy(step, group).wait_send()


def solution(mesh):
    n = mesh.shape["blk"]

    def on_device(positive_row, negative_row):
        size = positive_row.shape[0]
        chips = n // 2
        holders = min(chips, size // PIECE)
        dma = pltpu.SemaphoreType.DMA
        vmem = pl.BlockSpec(memory_space=pltpu.VMEM)
        hbm = pl.BlockSpec(memory_space=pltpu.HBM)
        return pl.pallas_call(
            functools.partial(kernel, n),
            out_shape=(pltpu.VMEM((size, size), jnp.float32),) * 2,
            in_specs=[hbm, hbm],
            out_specs=(vmem, vmem),
            scratch_shapes=[
                pltpu.VMEM((size, size), jnp.float32),
                pltpu.VMEM((size, size), jnp.float32),
                pltpu.VMEM((2, size, size), jnp.float32),
                pltpu.VMEM((2, size, size), jnp.float32),
                pltpu.VMEM((STEPS, size, size), jnp.float32),
                pltpu.VMEM((4, 2, size, size), jnp.bfloat16),
                pltpu.VMEM((4, size, size), jnp.float32),
                dma((2,)), dma((STEPS, holders)), dma((STEPS, chips)), dma((STEPS, holders)),
                dma((STEPS, GROUPS)), dma((STEPS, GROUPS)),
                dma((2,)), dma((2,)), dma, dma, dma((2,)), dma((2,)),
            ],
            compiler_params=pltpu.CompilerParams(
                collective_id=0, has_side_effects=True, vmem_limit_bytes=64000000),
        )(positive_row, negative_row)

    spec = (P(None, "blk"), P(None, "blk"))
    return jax.shard_map(on_device, mesh=mesh, in_specs=spec, out_specs=spec, check_vma=False)
```
